32 devices in a mesh: groups: 2 (over y), particle: 4 (over z), slab: 2 (over x), rep: 2 (over core).
Axes of the slice: x: 2, y: 2, z: 4, core: 2. Of those that a mesh axis runs over, the one named last changes fastest.
Arguments:
- images: float32 [64, 384, 384], P(('groups', 'particle', 'slab', 'rep')), parts along dimension 0, may hold values from -6 to 6
- poses: int32 [64], P(('groups', 'particle', 'slab', 'rep')), parts along dimension 0, may hold values from 0 to 31
- plane_index: int32 [32, 2, 4, 9], P(None, 'slab'), may hold values from 0 to 2
- plane_weight: float32 [32, 2, 4, 9], P(None, 'slab'), may hold values from 0.05 to 1
- shell_counts: int32 [576], P('groups'), parts along dimension 0, may hold values from 8 to 31
Outputs:
- volume: float32 [16, 384, 384], P(('groups', 'slab'), ('particle', 'rep')), parts along dimension 0
The draws below stay inside these ranges and needn't reach their ends.
There are 2 independent parts, one for each index of `groups`. The reference program is written for one: setup_inputs(seed, part) draws one part's arguments, and reference() takes and returns one part's arrays. A program takes and returns all parts, laid end to end along the dimension named above; an argument that names none is the same for every part. Nothing has to cross between parts.
All inputs are finite; a program needn't handle non-finite values.
Results may differ from the reference program's by a relative error of at most 0.0065.
Values may be sent and summed in bfloat16 or wider, within the bound.
A program may use at most 64 MiB of HBM per device.

```python
import math
import jax
import jax.numpy as jnp
from jax import lax

BOX = 384
ZS = 3
POSES = 32
ENTRIES = 4
TSIDE = 3
TILES = 9
SLABS = 2
IMAGES = 32
ZW = 6
OZ = 8
SHELLS = 288


def place_ends(drawn, rng, smallest, top_value):
    dims = drawn.shape
    index_at = [jax.random.randint(jax.random.fold_in(rng, axis), (), 0, dims[axis]) for axis in range(len(dims))]
    drawn = drawn.at[tuple(index_at)].set(smallest)
    longest = dims.index(max(dims))
    index_at[longest] = (index_at[longest] + 1) % dims[longest]
    return drawn.at[tuple(index_at)].set(top_value)


def level_of(stream_key, shape, cuts, least, top_value):
    def one(position, shards_of):
        draws = jax.random.uniform(jax.random.fold_in(jax.random.fold_in(stream_key, 6), position), (shards_of,), jnp.float32, least / len(cuts), top_value / len(cuts))
        return jnp.repeat(jnp.exp(draws), shape[position] // shards_of).reshape((-1,) + (1,) * (len(shape) - position - 1))

    level = one(*cuts[0])
    for cut in cuts[1:]:
        level = level * one(*cut)
    return level


def gaussian(stream_key, shape, scale, most, shards=(), kind=jnp.bfloat16):
    level = level_of(stream_key, shape, shards, -0.22, 0.18) if shards else 1.0
    drawn = jax.random.normal(stream_key, shape, jnp.float32) * scale * level
    return jnp.minimum(jnp.maximum(drawn, -most), most).astype(kind)


def setup_inputs(seed: int = 0, part: int = 0) -> dict:
    key_list = jax.random.split(jax.random.key(seed), 6)
    part_splits = jax.random.split(jax.random.fold_in(key_list[5], part), 6)
    return {
        "images": gaussian(part_splits[0], (IMAGES, BOX, BOX), 1.0, 6.0, ((0, 16),), jnp.float32),
        "poses": place_ends(jax.random.randint(part_splits[1], (IMAGES,), 0, POSES), jax.random.fold_in(part_splits[1], 1), 0, POSES - 1).astype(jnp.int32),
        "plane_index": place_ends(jax.random.randint(key_list[2], (POSES, SLABS, ENTRIES, TILES), 0, ZS), jax.random.fold_in(key_list[2], 1), 0, ZS - 1).astype(jnp.int32),
        "plane_weight": jnp.clip(0.05 + 0.95 * jax.random.uniform(key_list[3], (POSES, SLABS, ENTRIES, TILES), jnp.float32) ** level_of(key_list[3], (POSES, SLABS, ENTRIES, TILES), ((1, 2),), -0.2, 0.2), 0.05, 1.0),
        "shell_counts": place_ends(jax.random.randint(part_splits[4], (SHELLS,), IMAGES // 4, IMAGES), jax.random.fold_in(part_splits[4], 1), IMAGES // 4, IMAGES - 1).astype(jnp.int32),
    }


def phase_table(freq_list, positions, box_size):
    product = freq_list[:, None] * positions[None, :] % box_size
    return 2.0 * math.pi / box_size * product.astype(jnp.float32)

def centered(indices, box_size):
    return jnp.where(indices < box_size // 2, indices, indices - box_size)

def shell_index(squared):
    estimate = jnp.floor(jnp.sqrt(squared.astype(jnp.float32))).astype(jnp.int32)
    estimate = estimate - (estimate * estimate > squared).astype(jnp.int32)
    estimate = estimate + ((estimate + 1) * (estimate + 1) <= squared).astype(jnp.int32)
    return estimate

def grid_weight(positions, box_size):
    return jnp.sinc(centered(positions, box_size).astype(jnp.float32) / box_size) ** 2

def wide_dot(left, right):
    return jnp.dot(left.astype(jnp.float32), right.astype(jnp.float32), precision=lax.Precision.HIGHEST)

def reference(images, poses, plane_index, plane_weight, shell_counts):
    highest = lax.Precision.HIGHEST
    positions = jnp.arange(BOX, dtype=jnp.int32)
    angles = phase_table(positions, positions, BOX)
    root_box = math.sqrt(BOX)
    cos_table = (jnp.cos(angles) / root_box).astype(jnp.bfloat16)
    sin_table = (jnp.sin(angles) / root_box).astype(jnp.bfloat16)

    def spectrum(picture):
        rounded = picture.astype(jnp.bfloat16)
        real_part = wide_dot(rounded, cos_table).astype(jnp.bfloat16)
        imag_part = (-wide_dot(rounded, sin_table)).astype(jnp.bfloat16)
        spec_real = (wide_dot(cos_table, real_part) + wide_dot(sin_table, imag_part)).astype(jnp.bfloat16)
        spec_imag = (wide_dot(cos_table, imag_part) - wide_dot(sin_table, real_part)).astype(jnp.bfloat16)
        return jnp.stack([spec_real, spec_imag])
    spectra = lax.map(spectrum, images)
    chosen_index = plane_index[poses]
    chosen_weight = plane_weight[poses]
    planes = jnp.arange(ZS, dtype=jnp.int32)
    matches = (chosen_index[..., None] == planes).astype(jnp.float32)
    per_plane = lax.optimization_barrier(jnp.sum(matches * chosen_weight[..., None], axis=2))
    mixing = per_plane.transpose(1, 3, 2, 0).reshape(ZW, TSIDE, TSIDE, IMAGES).astype(jnp.bfloat16)
    tile_size = BOX // TSIDE
    tiled = spectra.reshape(IMAGES, 2, TSIDE, tile_size, TSIDE, tile_size)
    window = jnp.einsum('wabi,icaybx->wcaybx', mixing.astype(jnp.float32), tiled.astype(jnp.float32), precision=highest).reshape(ZW, 2, BOX, BOX)
    depth_freq = jnp.arange(ZW, dtype=jnp.int32) - ZW // 2
    frequencies = centered(positions, BOX)
    squared = depth_freq[:, None, None] ** 2 + frequencies[None, :, None] ** 2 + frequencies[None, None, :] ** 2
    inverse_root = 1.0 / jnp.sqrt(shell_counts.astype(jnp.float32))
    shell_scale = inverse_root[shell_index(squared)]
    normed = window * shell_scale[:, None]
    cosine = jnp.cos(angles) / root_box
    sine = jnp.sin(angles) / root_box
    real_x = jnp.einsum('zyk,kx->zyx', normed[:, 0], cosine, precision=highest) - jnp.einsum('zyk,kx->zyx', normed[:, 1], sine, precision=highest)
    imag_x = jnp.einsum('zyk,kx->zyx', normed[:, 0], sine, precision=highest) + jnp.einsum('zyk,kx->zyx', normed[:, 1], cosine, precision=highest)
    real_y = jnp.einsum('zkx,ky->zyx', real_x, cosine, precision=highest) - jnp.einsum('zkx,ky->zyx', imag_x, sine, precision=highest)
    imag_y = jnp.einsum('zkx,ky->zyx', real_x, sine, precision=highest) + jnp.einsum('zkx,ky->zyx', imag_x, cosine, precision=highest)
    out_rows = jnp.arange(OZ, dtype=jnp.int32) * (BOX // OZ)
    depth_angle = phase_table(depth_freq, out_rows, BOX)
    depth_cos = jnp.cos(depth_angle) / math.sqrt(ZW)
    depth_sin = jnp.sin(depth_angle) / math.sqrt(ZW)
    raw = jnp.einsum('zo,zyx->oxy', depth_cos, real_y, precision=highest) - jnp.einsum('zo,zyx->oxy', depth_sin, imag_y, precision=highest)
    correction = grid_weight(out_rows, BOX)[:, None, None] * grid_weight(positions, BOX)[None, :, None] * grid_weight(positions, BOX)[None, None, :]
    return raw / correction
```

```python
import functools
import math

import jax
import jax.numpy as jnp
import ml_dtypes
import numpy as np
from jax import lax
from jax.experimental import pallas as pl
from jax.experimental.pallas import tpu as pltpu
from jax.sharding import PartitionSpec as P

ZS = 3
OZS = 4
TSIDE = 3


def phase_table(freq_list, positions, box_size):
    product = freq_list[:, None] * positions[None, :] % box_size
    return 2.0 * math.pi / box_size * product.astype(jnp.float32)


def centered(indices, box_size):
    return jnp.where(indices < box_size // 2, indices, indices - box_size)


def shell_index(squared):
    estimate = jnp.floor(jnp.sqrt(squared.astype(jnp.float32))).astype(jnp.int32)
    estimate = estimate - (estimate * estimate > squared).astype(jnp.int32)
    estimate = estimate + ((estimate + 1) * (estimate + 1) <= squared).astype(jnp.int32)
    return estimate


def grid_weight(positions, box_size):
    return jnp.sinc(centered(positions, box_size).astype(jnp.float32) / box_size) ** 2


def spectra_of(pictures, cos_table, sin_table):
    box_size = cos_table.shape[0]
    cos_sin = jnp.concatenate([cos_table, sin_table], axis=1)
    table_pair = jnp.stack([cos_sin, jnp.concatenate([-sin_table, cos_table], axis=1)])

    def single(picture):
        section_one = jnp.dot(picture, cos_sin, preferred_element_type=jnp.float32)
        real_part = section_one[:, :box_size].astype(jnp.bfloat16)
        imag_part = (-section_one[:, box_size:]).astype(jnp.bfloat16)
        stacked = jnp.concatenate([real_part, imag_part], axis=0)
        return jnp.einsum(
            "aky,yx->akx", table_pair, stacked, preferred_element_type=jnp.float32
        ).astype(jnp.bfloat16)

    return lax.map(single, pictures)


def insert_images(running, spectra, pose_piece, local_index, local_weight):
    highest = lax.Precision.HIGHEST
    pose_total = local_index.shape[0]
    entry_total = local_index.shape[1]
    tile_total = local_index.shape[2]
    plane_total = running.shape[0]
    box_size = spectra.shape[-1]
    tile_size = box_size // TSIDE
    count = pose_piece.shape[0]
    onehot = (pose_piece[:, None] == jnp.arange(pose_total, dtype=jnp.int32)[None, :]).astype(
        jnp.float32
    )
    chosen_index = jnp.dot(
        onehot,
        local_index.reshape(pose_total, entry_total * tile_total).astype(jnp.float32),
        precision=highest,
    )
    chosen_weight = jnp.dot(
        onehot, local_weight.reshape(pose_total, entry_total * tile_total), precision=highest
    )
    chosen_index = chosen_index.reshape(count, entry_total, tile_total)
    chosen_weight = chosen_weight.reshape(count, entry_total, tile_total)
    planes = jnp.arange(plane_total).astype(jnp.float32)
    matches = (chosen_index[..., None] == planes).astype(jnp.float32)
    per_plane = jnp.sum(matches * chosen_weight[..., None], axis=1)
    mixing = (
        per_plane.transpose(2, 1, 0).reshape(plane_total, TSIDE, TSIDE, count).astype(jnp.bfloat16)
    )
    tiled = spectra.reshape(count, 2, TSIDE, tile_size, TSIDE, tile_size)
    added = jnp.einsum("zabi,icaybx->zcaybx", mixing, tiled, preferred_element_type=jnp.float32)
    return added.reshape(plane_total, 2, box_size, box_size)


def body(images, poses, plane_index, plane_weight, shell_counts):
    highest = lax.Precision.HIGHEST
    box_size = images.shape[-1]
    slab_index = lax.axis_index("slab")
    slab_total = lax.axis_size("slab")
    pencil_index = lax.axis_index(("particle", "rep"))
    positions = jnp.arange(box_size, dtype=jnp.int32)
    angles = phase_table(positions, positions, box_size)
    root_box = math.sqrt(box_size)
    cos_table = (jnp.cos(angles) / root_box).astype(jnp.bfloat16)
    sin_table = (jnp.sin(angles) / root_box).astype(jnp.bfloat16)
    local_index = plane_index[:, 0]
    local_weight = plane_weight[:, 0]
    empty_window = jnp.zeros((ZS, 2, box_size, box_size), jnp.float32)
    partial_value = insert_images(
        empty_window,
        spectra_of(
            lax.all_gather(images.astype(jnp.bfloat16), "slab", axis=0, tiled=True),
            cos_table,
            sin_table,
        ),
        lax.all_gather(poses, "slab", axis=0, tiled=True),
        local_index,
        local_weight,
    )
    summed = lax.psum_scatter(partial_value, ("particle", "rep"), scatter_dimension=2, tiled=True)
    row_total = summed.shape[2]
    window_planes = ZS * slab_total
    depth_freq = slab_index * ZS + jnp.arange(ZS, dtype=jnp.int32) - window_planes // 2
    row_freq = centered(pencil_index * row_total + jnp.arange(row_total, dtype=jnp.int32), box_size)
    column_freq = centered(positions, box_size)
    inverse_root = 1.0 / jnp.sqrt(shell_counts.astype(jnp.float32))
    shell_ids = jnp.arange(inverse_root.shape[0], dtype=jnp.int32)

    def plane_scale(depth_value):
        squared = depth_value * depth_value + row_freq[:, None] ** 2 + column_freq[None, :] ** 2
        member = (shell_index(squared)[:, :, None] == shell_ids[None, None, :]).astype(jnp.float32)
        return jnp.dot(member, inverse_root, precision=highest)

    shell_scale = lax.map(plane_scale, depth_freq)
    normed = summed * shell_scale[:, None]
    cosine = jnp.cos(angles) / root_box
    sine = jnp.sin(angles) / root_box
    inverse_table = jnp.stack([jnp.stack([cosine, sine]), jnp.stack([-sine, cosine])])
    across = jnp.einsum("zcyk,cakx->zaxy", normed, inverse_table, precision=highest)
    pencils = lax.all_to_all(across, ("particle", "rep"), split_axis=2, concat_axis=3, tiled=True)
    pencil_lines = jnp.einsum("zcxk,caky->zaxy", pencils, inverse_table, precision=highest)
    column_total = pencil_lines.shape[2]
    out_planes = OZS * slab_total
    spacing = box_size // out_planes
    own_rows = slab_index * OZS + jnp.arange(OZS, dtype=jnp.int32)
    depth_angle = phase_table(
        depth_freq, jnp.arange(lax.axis_size("slab") * OZS, dtype=jnp.int32) * spacing, box_size
    )
    depth_cos = jnp.cos(depth_angle) / math.sqrt(window_planes)
    depth_sin = jnp.sin(depth_angle) / math.sqrt(window_planes)
    raw = lax.psum_scatter(
        jnp.einsum("zo,zxy->oxy", depth_cos, pencil_lines[:, 0], precision=highest)
        - jnp.einsum("zo,zxy->oxy", depth_sin, pencil_lines[:, 1], precision=highest),
        "slab",
        scatter_dimension=0,
        tiled=True,
    )
    column_pos = pencil_index * column_total + jnp.arange(column_total, dtype=jnp.int32)
    correction = (
        grid_weight(own_rows * spacing, box_size)[:, None, None]
        * grid_weight(column_pos, box_size)[None, :, None]
        * grid_weight(positions, box_size)[None, None, :]
    )
    return raw / correction


BOX = 384
DEVS = 16
ROWS = BOX // DEVS
LINES = 8
XS = BOX // LINES
FREQS = 7
MESH = pl.DeviceIdType.MESH
F32 = jnp.float32
BF16 = jnp.bfloat16


def host_tables():
    k = np.arange(BOX)
    theta = 2.0 * np.pi * ((k[:, None] * k[None, :]) % BOX) / BOX
    cos, sin = np.cos(theta) / math.sqrt(BOX), np.sin(theta) / math.sqrt(BOX)
    q = np.where(k < BOX // 2, k, k - BOX)
    weight = np.sinc(q / BOX) ** 2
    over_x = np.block([[cos, -sin], [sin, cos]])
    both = np.stack([np.concatenate([cos, sin], 1), np.concatenate([-sin, cos], 1)])
    over_y = both.reshape(2, DEVS, ROWS, 2 * BOX).transpose(1, 0, 2, 3).reshape(2 * BOX, 2 * BOX)
    inverse = np.stack([np.concatenate([cos, -sin], 0), np.concatenate([sin, cos], 0)], 1) / weight
    inverse = inverse.reshape(2 * BOX, 2, LINES, XS).transpose(0, 2, 1, 3).reshape(2 * BOX, LINES, 2 * XS)
    back_x = np.zeros((2 * BOX, LINES, 128))
    back_x[:, :, : 2 * XS] = inverse
    back_y = np.concatenate([cos / weight, sin / weight], 1)
    place = np.zeros((FREQS, 256, 32))
    for n in range(FREQS):
        for side, kz in enumerate((n - 3, 3 - n)):
            if kz <= 2:
                slab, plane = divmod(kz + 3, ZS)
                for t in range(9):
                    place[n, slab * 128 + plane * 9 + t, side * 9 + t] = 1.0
    tables = over_x, over_y, back_x.reshape(2 * BOX, LINES * 128), back_y, place
    return [t.astype(np.float32).astype(ml_dtypes.bfloat16) for t in tables], weight


def device_number():
    return lax.axis_index("particle") * 4 + lax.axis_index("slab") * 2 + lax.axis_index("rep")


def scale_kernel(counts_ref, out_ref):
    me = device_number()
    ky = lax.broadcasted_iota(jnp.int32, (ROWS, 128), 0) + me * ROWS
    ky = jnp.where(ky < BOX // 2, ky, ky - BOX)
    root = lax.rsqrt(counts_ref[...].astype(F32))
    for tile in range(3):
        kx = lax.broadcasted_iota(jnp.int32, (ROWS, 128), 1) + tile * 128
        kx = jnp.where(kx < BOX // 2, kx, kx - BOX)
        for kz in range(4):
            r2 = ky * ky + kx * kx + kz * kz
            s = jnp.sqrt(r2.astype(F32)).astype(jnp.int32)
            s = s - (s * s > r2).astype(jnp.int32)
            s = s + ((s + 1) * (s + 1) <= r2).astype(jnp.int32)
            low = s % 128
            total = jnp.zeros((ROWS, 128), F32)
            for part in range(3):
                line = jnp.broadcast_to(root[part : part + 1, :], (ROWS, 128))
                got = jnp.take_along_axis(line, low, axis=1, mode="promise_in_bounds")
                total = jnp.where(s // 128 == part, got, total)
            out_ref[kz * ROWS : (kz + 1) * ROWS, tile * 128 : (tile + 1) * 128] = total


def main_kernel(
    weight,
    img_ref, hot_ref, tab_ref, scale_ref, w1_ref, w2_ref, w3_ref, w4_ref, place_ref,
    out_ref,
    hots, tabs, hbuf, gbuf, rbuf, gf, coef, qf, zbuf, zrecv,
    hot_send, hot_recv, tab_send, tab_recv, g_send, g_recv, z_send, z_recv,
):
    me = device_number()
    group = lax.axis_index("groups")
    my_slab = lax.axis_index("slab")

    def where_is(d):
        return (group, d // 4, (d // 2) % 2, d % 2)

    def peer(n):
        return (me + n) % DEVS

    barrier = pltpu.get_barrier_semaphore()
    for n in range(1, DEVS):
        pl.semaphore_signal(barrier, inc=1, device_id=where_is(peer(n)), device_id_type=MESH)

    hots[me] = hot_ref[...]
    tabs[my_slab] = tab_ref[...]
    pair = jnp.concatenate([img_ref[0].astype(BF16), img_ref[1].astype(BF16)], axis=1)
    first = jnp.dot(pair, w1_ref[...], preferred_element_type=F32).astype(BF16)
    hbuf[0:BOX, :] = first[:, :BOX]
    hbuf[BOX:, :] = first[:, BOX:]

    pl.semaphore_wait(barrier, DEVS - 1)

    def hot_copy(slot, d):
        return pltpu.make_async_remote_copy(
            src_ref=hot_ref, dst_ref=hots.at[slot], send_sem=hot_send.at[d], recv_sem=hot_recv.at[slot],
            device_id=where_is(d), device_id_type=MESH)

    def tab_copy(slot):
        return pltpu.make_async_remote_copy(
            src_ref=tab_ref, dst_ref=tabs.at[slot], send_sem=tab_send, recv_sem=tab_recv,
            device_id=where_is(me + 2 - 4 * my_slab), device_id_type=MESH)

    def g_copy(slot, d):
        return pltpu.make_async_remote_copy(
            src_ref=gbuf.at[d], dst_ref=rbuf.at[slot], send_sem=g_send.at[d], recv_sem=g_recv.at[slot],
            device_id=where_is(d), device_id_type=MESH)

    def z_copy(slot, d):
        return pltpu.make_async_remote_copy(
            src_ref=zbuf.at[d], dst_ref=zrecv.at[slot], send_sem=z_send.at[d], recv_sem=z_recv.at[slot],
            device_id=where_is(d), device_id_type=MESH)

    tab_copy(my_slab).start()
    for n in range(1, DEVS):
        hot_copy(me, peer(n)).start()

    my_quad = me // 4
    my_place = me % 4
    for step in (2, 1, 3, 0):
        quad = (my_quad + step) % 4
        rows = w2_ref[pl.ds(pl.multiple_of(quad * 192, 192), 192), :]
        made = jnp.dot(rows, hbuf[...], preferred_element_type=F32).astype(BF16)
        gbuf[pl.ds(quad * 4, 4)] = made.reshape(4, 2 * ROWS, BOX)
        for n in range(4 if step else 3):
            d = quad * 4 + (n if step else (my_place + 1 + n) % 4)
            g_copy(me, d).start()
    rbuf[me] = gbuf[me]

    tab_copy(1 - my_slab).wait()
    for n in range(1, DEVS):
        hot_copy(peer(n), peer(n)).wait()
    hot = jnp.concatenate([hots[:, 0, :], hots[:, 1, :]], axis=0)[:, :32].astype(BF16)
    chosen = jnp.concatenate(
        [jnp.dot(hot, tabs[s], preferred_element_type=F32).astype(BF16) for s in range(2)], axis=1)
    mixed = jnp.concatenate(
        [jnp.dot(chosen, place_ref[n], preferred_element_type=F32).astype(BF16) for n in range(FREQS)], axis=0)
    lane = lax.broadcasted_iota(jnp.int32, (32, BOX), 1)
    entry = lax.broadcasted_iota(jnp.int32, (32, BOX), 0)
    tile = lane // 128
    mirror = jnp.where(lane == 0, 0, (BOX - lane) // 128)
    for ch in range(3):
        for v in range(2):
            ky = me * ROWS + ch * 8 + (1 - v)
            at = ky // 128 * 3 + tile
            mirror_at = 9 + (BOX - ky) % BOX // 128 * 3 + mirror
            select = ((entry == at) | (entry == mirror_at)).astype(F32).astype(BF16)
            coef[ch, v] = jnp.dot(mixed, select, preferred_element_type=F32)

    for n in range(1, DEVS):
        g_copy(peer(n), peer(n)).wait()
    gf[...] = rbuf[...].astype(F32)

    row_zero = lax.broadcasted_iota(jnp.int32, (8, BOX), 0) == 0

    def per_group(ch, _):
        base = pl.multiple_of(ch * 8, 8)

        def per_pair(p, sums):
            gr = gf[p, pl.ds(base, 8), :]
            gi = gf[p, pl.ds(base + ROWS, 8), :]
            new = []
            for n in range(FREQS):
                one = jnp.where(row_zero, coef[ch, 1, pl.ds(n * 32 + p, 1), :], coef[ch, 0, pl.ds(n * 32 + p, 1), :])
                two = jnp.where(
                    row_zero, coef[ch, 1, pl.ds(n * 32 + 16 + p, 1), :], coef[ch, 0, pl.ds(n * 32 + 16 + p, 1), :])
                new.append(sums[2 * n] + (one * gr + two * gi))
                new.append(sums[2 * n + 1] + (one * gi - two * gr))
            return tuple(new)

        sums = lax.fori_loop(0, DEVS, per_pair, tuple(jnp.zeros((8, BOX), F32) for _ in range(2 * FREQS)))
        scales = [scale_ref[pl.ds(base + ROWS * j, 8), :] for j in range(4)]
        re = [sums[2 * n] * scales[abs(n - 3)] for n in range(FREQS)]
        im = [sums[2 * n + 1] * scales[abs(n - 3)] for n in range(FREQS)]
        even = [(re[3 + j] + re[3 - j], im[3 + j] + im[3 - j]) for j in range(1, 4)]
        odd = [(re[3 + j] - re[3 - j], im[3 + j] - im[3 - j]) for j in range(1, 4)]
        for o in range(8):
            factor = 0.5 / math.sqrt(6.0) / float(weight[o * 48])
            out_re, out_im = re[3] * factor, im[3] * factor
            for j in range(1, 4):
                c = factor * math.cos(2.0 * math.pi * (j * o % 8) / 8)
                s = factor * math.sin(2.0 * math.pi * (j * o % 8) / 8)
                out_re = out_re + (c * even[j - 1][0] - s * odd[j - 1][1])
                out_im = out_im + (c * even[j - 1][1] + s * odd[j - 1][0])
            qf[pl.ds(base + o * ROWS, 8), 0:BOX] = out_re
            qf[pl.ds(base + o * ROWS, 8), BOX:] = out_im
        return 0

    lax.fori_loop(0, 3, per_group, 0)

    for s in range(2):
        part = qf[s * 96 : (s + 1) * 96, :].astype(BF16)
        lines = jnp.dot(part, w3_ref[...], preferred_element_type=F32).astype(BF16)
        for q in range(LINES):
            zbuf[q // 2 * 4 + s * 2 + q % 2] = lines[:, q * 128 : (q + 1) * 128]
    for n in (8, 7, 9, 6, 10, 5, 11, 4, 12, 3, 13, 2, 14, 1, 15):
        z_copy(me, peer(n)).start()
    zrecv[me] = zbuf[me]
    for n in range(1, DEVS):
        z_copy(peer(n), peer(n)).wait()
    got = zrecv[...].astype(F32)
    for o in range(4):
        column = got[:, o * ROWS : (o + 1) * ROWS, :].reshape(BOX, 128).astype(BF16)
        res = lax.dot_general(column, w4_ref[...], (((0,), (0,)), ((), ())), preferred_element_type=F32)
        out_ref[o] = res[0:XS, :BOX] - res[XS : 2 * XS, BOX:]


def fused(images, poses, plane_index, plane_weight, shell_counts):
    tables, weight = host_tables()
    vmem = pl.BlockSpec(memory_space=pltpu.VMEM)
    counts = jnp.pad(shell_counts, (0, BOX - shell_counts.shape[0]), constant_values=1).reshape(3, 128)
    scale = pl.pallas_call(
        scale_kernel,
        out_shape=jax.ShapeDtypeStruct((4 * ROWS, BOX), F32),
        in_specs=[vmem],
        out_specs=vmem,
        name="shell_scale",
    )(counts)
    hot = (poses[:, None] == jnp.arange(128, dtype=jnp.int32)[None, :]).astype(F32)
    hot = jnp.pad(hot, ((0, 6), (0, 0)))
    index, entries = plane_index[:, 0], plane_weight[:, 0]
    planes = jnp.arange(ZS, dtype=jnp.int32)[None, :, None, None]
    table = jnp.sum(jnp.where(index[:, None] == planes, entries[:, None], 0.0), axis=2)
    table = jnp.pad(table.reshape(32, 27).astype(BF16), ((0, 0), (0, 101)))
    return pl.pallas_call(
        functools.partial(main_kernel, weight),
        out_shape=jax.ShapeDtypeStruct((4, XS, BOX), F32),
        in_specs=[vmem] * 9,
        out_specs=vmem,
        scratch_shapes=[
            pltpu.VMEM((DEVS, 8, 128), F32),
            pltpu.VMEM((2, 32, 128), BF16),
            pltpu.VMEM((2 * BOX, BOX), BF16),
            pltpu.VMEM((DEVS, 2 * ROWS, BOX), BF16),
            pltpu.VMEM((DEVS, 2 * ROWS, BOX), BF16),
            pltpu.VMEM((DEVS, 2 * ROWS, BOX), F32),
            pltpu.VMEM((3, 2, FREQS * 32, BOX), F32),
            pltpu.VMEM((8 * ROWS, 2 * BOX), F32),
            pltpu.VMEM((DEVS, 96, 128), BF16),
            pltpu.VMEM((DEVS, 96, 128), BF16),
            pltpu.SemaphoreType.DMA((DEVS,)),
            pltpu.SemaphoreType.DMA((DEVS,)),
            pltpu.SemaphoreType.DMA,
            pltpu.SemaphoreType.DMA,
            pltpu.SemaphoreType.DMA((DEVS,)),
            pltpu.SemaphoreType.DMA((DEVS,)),
            pltpu.SemaphoreType.DMA((DEVS,)),
            pltpu.SemaphoreType.DMA((DEVS,)),
        ],
        compiler_params=pltpu.CompilerParams(
            collective_id=0, has_side_effects=True, vmem_limit_bytes=48 * 2**20
        ),
        name="reconstruct",
    )(images, hot, table, scale, *[jnp.asarray(t) for t in tables])


def solution(mesh):
    small = (mesh.shape["particle"], mesh.shape["slab"], mesh.shape["rep"]) == (4, 2, 2)
    in_specs = (
        P(("groups", "particle", "slab", "rep"), None, None),
        P(("groups", "particle", "slab", "rep")),
        P(None, "slab", None, None),
        P(None, "slab", None, None),
        P("groups"),
    )
    out_specs = P(("groups", "slab"), ("particle", "rep"), None)
    return jax.shard_map(fused if small else body, mesh=mesh, in_specs=in_specs, out_specs=out_specs, check_vma=False)
```

```python
import functools
import math

import jax
import jax.numpy as jnp
import ml_dtypes
import numpy as np
from jax import lax
from jax.experimental import pallas as pl
from jax.experimental.pallas import tpu as pltpu
from jax.sharding import PartitionSpec as P

ZS = 3
OZS = 4
TSIDE = 3


def phase_table(freq_list, positions, box_size):
    product = freq_list[:, None] * positions[None, :] % box_size
    return 2.0 * math.pi / box_size * product.astype(jnp.float32)


def centered(indices, box_size):
    return jnp.where(indices < box_size // 2, indices, indices - box_size)


def shell_index(squared):
    estimate = jnp.floor(jnp.sqrt(squared.astype(jnp.float32))).astype(jnp.int32)
    estimate = estimate - (estimate * estimate > squared).astype(jnp.int32)
    estimate = estimate + ((estimate + 1) * (estimate + 1) <= squared).astype(jnp.int32)
    return estimate


def grid_weight(positions, box_size):
    return jnp.sinc(centered(positions, box_size).astype(jnp.float32) / box_size) ** 2


def spectra_of(pictures, cos_table, sin_table):
    box_size = cos_table.shape[0]
    cos_sin = jnp.concatenate([cos_table, sin_table], axis=1)
    table_pair = jnp.stack([cos_sin, jnp.concatenate([-sin_table, cos_table], axis=1)])

    def single(picture):
        section_one = jnp.dot(picture, cos_sin, preferred_element_type=jnp.float32)
        real_part = section_one[:, :box_size].astype(jnp.bfloat16)
        imag_part = (-section_one[:, box_size:]).astype(jnp.bfloat16)
        stacked = jnp.concatenate([real_part, imag_part], axis=0)
        return jnp.einsum(
            "aky,yx->akx", table_pair, stacked, preferred_element_type=jnp.float32
        ).astype(jnp.bfloat16)

    return lax.map(single, pictures)


def insert_images(running, spectra, pose_piece, local_index, local_weight):
    highest = lax.Precision.HIGHEST
    pose_total = local_index.shape[0]
    entry_total = local_index.shape[1]
    tile_total = local_index.shape[2]
    plane_total = running.shape[0]
    box_size = spectra.shape[-1]
    tile_size = box_size // TSIDE
    count = pose_piece.shape[0]
    onehot = (pose_piece[:, None] == jnp.arange(pose_total, dtype=jnp.int32)[None, :]).astype(
        jnp.float32
    )
    chosen_index = jnp.dot(
        onehot,
        local_index.reshape(pose_total, entry_total * tile_total).astype(jnp.float32),
        precision=highest,
    )
    chosen_weight = jnp.dot(
        onehot, local_weight.reshape(pose_total, entry_total * tile_total), precision=highest
    )
    chosen_index = chosen_index.reshape(count, entry_total, tile_total)
    chosen_weight = chosen_weight.reshape(count, entry_total, tile_total)
    planes = jnp.arange(plane_total).astype(jnp.float32)
    matches = (chosen_index[..., None] == planes).astype(jnp.float32)
    per_plane = jnp.sum(matches * chosen_weight[..., None], axis=1)
    mixing = (
        per_plane.transpose(2, 1, 0).reshape(plane_total, TSIDE, TSIDE, count).astype(jnp.bfloat16)
    )
    tiled = spectra.reshape(count, 2, TSIDE, tile_size, TSIDE, tile_size)
    added = jnp.einsum("zabi,icaybx->zcaybx", mixing, tiled, preferred_element_type=jnp.float32)
    return added.reshape(plane_total, 2, box_size, box_size)


def body(images, poses, plane_index, plane_weight, shell_counts):
    highest = lax.Precision.HIGHEST
    box_size = images.shape[-1]
    slab_index = lax.axis_index("slab")
    slab_total = lax.axis_size("slab")
    pencil_index = lax.axis_index(("particle", "rep"))
    positions = jnp.arange(box_size, dtype=jnp.int32)
    angles = phase_table(positions, positions, box_size)
    root_box = math.sqrt(box_size)
    cos_table = (jnp.cos(angles) / root_box).astype(jnp.bfloat16)
    sin_table = (jnp.sin(angles) / root_box).astype(jnp.bfloat16)
    local_index = plane_index[:, 0]
    local_weight = plane_weight[:, 0]
    empty_window = jnp.zeros((ZS, 2, box_size, box_size), jnp.float32)
    partial_value = insert_images(
        empty_window,
        spectra_of(
            lax.all_gather(images.astype(jnp.bfloat16), "slab", axis=0, tiled=True),
            cos_table,
            sin_table,
        ),
        lax.all_gather(poses, "slab", axis=0, tiled=True),
        local_index,
        local_weight,
    )
    summed = lax.psum_scatter(partial_value, ("particle", "rep"), scatter_dimension=2, tiled=True)
    row_total = summed.shape[2]
    window_planes = ZS * slab_total
    depth_freq = slab_index * ZS + jnp.arange(ZS, dtype=jnp.int32) - window_planes // 2
    row_freq = centered(pencil_index * row_total + jnp.arange(row_total, dtype=jnp.int32), box_size)
    column_freq = centered(positions, box_size)
    inverse_root = 1.0 / jnp.sqrt(shell_counts.astype(jnp.float32))
    shell_ids = jnp.arange(inverse_root.shape[0], dtype=jnp.int32)

    def plane_scale(depth_value):
        squared = depth_value * depth_value + row_freq[:, None] ** 2 + column_freq[None, :] ** 2
        member = (shell_index(squared)[:, :, None] == shell_ids[None, None, :]).astype(jnp.float32)
        return jnp.dot(member, inverse_root, precision=highest)

    shell_scale = lax.map(plane_scale, depth_freq)
    normed = summed * shell_scale[:, None]
    cosine = jnp.cos(angles) / root_box
    sine = jnp.sin(angles) / root_box
    inverse_table = jnp.stack([jnp.stack([cosine, sine]), jnp.stack([-sine, cosine])])
    across = jnp.einsum("zcyk,cakx->zaxy", normed, inverse_table, precision=highest)
    pencils = lax.all_to_all(across, ("particle", "rep"), split_axis=2, concat_axis=3, tiled=True)
    pencil_lines = jnp.einsum("zcxk,caky->zaxy", pencils, inverse_table, precision=highest)
    column_total = pencil_lines.shape[2]
    out_planes = OZS * slab_total
    spacing = box_size // out_planes
    own_rows = slab_index * OZS + jnp.arange(OZS, dtype=jnp.int32)
    depth_angle = phase_table(
        depth_freq, jnp.arange(lax.axis_size("slab") * OZS, dtype=jnp.int32) * spacing, box_size
    )
    depth_cos = jnp.cos(depth_angle) / math.sqrt(window_planes)
    depth_sin = jnp.sin(depth_angle) / math.sqrt(window_planes)
    raw = lax.psum_scatter(
        jnp.einsum("zo,zxy->oxy", depth_cos, pencil_lines[:, 0], precision=highest)
        - jnp.einsum("zo,zxy->oxy", depth_sin, pencil_lines[:, 1], precision=highest),
        "slab",
        scatter_dimension=0,
        tiled=True,
    )
    column_pos = pencil_index * column_total + jnp.arange(column_total, dtype=jnp.int32)
    correction = (
        grid_weight(own_rows * spacing, box_size)[:, None, None]
        * grid_weight(column_pos, box_size)[None, :, None]
        * grid_weight(positions, box_size)[None, None, :]
    )
    return raw / correction


BOX = 384
DEVS = 16
ROWS = BOX // DEVS
LINES = 8
XS = BOX // LINES
FREQS = 7
MESH = pl.DeviceIdType.MESH
F32 = jnp.float32
BF16 = jnp.bfloat16


def ky_of(me, row):
    back = row >= 12
    j = row - 4 * (back & (row < 16)) - 16 * (row >= 16)
    slot = me * 12 + j
    ky = slot + ((slot >= 128) & (slot < 132)) - 4 * (slot == 132)
    return ky + back * (BOX - 2 * ky - (BOX // 2) * (slot == 0))


def host_tables():
    k = np.arange(BOX)
    theta = 2.0 * np.pi * ((k[:, None] * k[None, :]) % BOX) / BOX
    cos, sin = np.cos(theta) / math.sqrt(BOX), np.sin(theta) / math.sqrt(BOX)
    q = np.where(k < BOX // 2, k, k - BOX)
    weight = np.sinc(q / BOX) ** 2
    over_x = np.block([[cos, -sin], [sin, cos]])
    both = np.stack([np.concatenate([cos, sin], 1), np.concatenate([-sin, cos], 1)])
    order = ky_of(np.arange(DEVS)[:, None], np.arange(ROWS)[None, :])
    over_y = both[:, order].transpose(1, 0, 2, 3).reshape(2 * BOX, 2 * BOX)
    def lines(table):
        padded = np.zeros((2 * BOX, LINES, 64))
        padded[:, :, :XS] = (table / weight).reshape(2 * BOX, LINES, XS)
        return padded.reshape(2 * BOX, LINES * 64)

    back_x = np.stack([lines(np.concatenate([cos, -sin], 0)), lines(np.concatenate([sin, cos], 0))])
    positive = order[:, :12]
    parts = [cos[positive] / weight, sin[positive] / weight]
    parts[1][0, 0] = -cos[BOX // 2] / weight
    basis = np.concatenate(parts, 2)
    back_y = np.zeros((2, 2, DEVS, 8, 2 * BOX))
    for parity in range(2):
        back_y[parity, 0] = basis[:, :8]
        back_y[parity, 1, :, 4 * parity : 4 * parity + 4] = basis[:, 8:]
    back_y = back_y.reshape(2, 2 * DEVS * 8, 2 * BOX)
    place = np.zeros((FREQS, 256, 32))
    for n in range(FREQS):
        for side, kz in enumerate((n - 3, 3 - n)):
            if kz <= 2:
                slab, plane = divmod(kz + 3, ZS)
                for t in range(9):
                    place[n, slab * 128 + plane * 9 + t, side * 9 + t] = 1.0
    tables = over_x, over_y, back_x, back_y, place
    return [t.astype(np.float32).astype(ml_dtypes.bfloat16) for t in tables], weight


def device_number():
    return lax.axis_index("particle") * 4 + lax.axis_index("slab") * 2 + lax.axis_index("rep")


def scale_kernel(counts_ref, out_ref):
    me = device_number()
    row = lax.broadcasted_iota(jnp.int32, (ROWS, 128), 0)
    back = row >= 12
    slot = me * 12 + jnp.where(back, jnp.where(row < 16, row - 4, row - 16), row)
    ky = jnp.where((slot >= 128) & (slot < 132), slot + 1, jnp.where(slot == 132, 128, slot))
    ky = jnp.where(back & (slot == 0), BOX // 2, ky)
    filled = jnp.concatenate([counts_ref[...], jnp.ones((1, BOX - counts_ref.shape[1]), jnp.int32)], axis=1)
    root = lax.rsqrt(filled.astype(F32))
    for tile in range(3):
        kx = lax.broadcasted_iota(jnp.int32, (ROWS, 128), 1) + tile * 128
        kx = jnp.where(kx < BOX // 2, kx, kx - BOX)
        for kz in range(4):
            r2 = ky * ky + kx * kx + kz * kz
            s = jnp.sqrt(r2.astype(F32)).astype(jnp.int32)
            s = s - (s * s > r2).astype(jnp.int32)
            s = s + ((s + 1) * (s + 1) <= r2).astype(jnp.int32)
            low = s % 128
            total = jnp.zeros((ROWS, 128), F32)
            for part in range(3):
                line = jnp.broadcast_to(root[:, part * 128 : (part + 1) * 128], (ROWS, 128))
                got = jnp.take_along_axis(line, low, axis=1, mode="promise_in_bounds")
                total = jnp.where(s // 128 == part, got, total)
            out_ref[kz * ROWS : (kz + 1) * ROWS, tile * 128 : (tile + 1) * 128] = total


def main_kernel(
    weight,
    img_hbm, poses_ref, index_ref, entry_ref, scale_ref, w1_hbm, w2_hbm, w3_hbm, w4_hbm, place_hbm,
    out_ref,
    img_ref, w1_ref, w2_ref, w3_ref, w4_ref, place_ref, hot_ref, tab_ref,
    hots, tabs, hbuf, gbuf, rbuf, gf, coef, qf, zbuf, zrecv,
    hot_send, hot_recv, tab_send, tab_recv, g_send, g_recv, z_send, z_recv, load_sem,
):
    me = device_number()
    group = lax.axis_index("groups")
    my_slab = lax.axis_index("slab")

    def where_is(d):
        return (group, d // 4, (d // 2) % 2, d % 2)

    def peer(n):
        return (me + n) % DEVS

    barrier = pltpu.get_barrier_semaphore()
    for n in range(1, DEVS):
        pl.semaphore_signal(barrier, inc=1, device_id=where_is(peer(n)), device_id_type=MESH)

    loads = [
        pltpu.make_async_copy(src, dst, load_sem.at[n])
        for n, (src, dst) in enumerate([
            (img_hbm, img_ref), (w1_hbm, w1_ref), (w2_hbm, w2_ref), (place_hbm, place_ref),
            (w3_hbm, w3_ref), (w4_hbm, w4_ref)])
    ]
    for load in loads:
        load.start()

    spot = lax.broadcasted_iota(jnp.int32, (8, 128), 1)
    line = lax.broadcasted_iota(jnp.int32, (8, 128), 0)
    hot_ref[...] = (spot == jnp.where(line == 0, poses_ref[0], poses_ref[1])).astype(F32)
    planes = []
    for z in range(ZS):
        total = jnp.zeros((32, 9), F32)
        for e in range(4):
            total = total + jnp.where(index_ref[e] == z, entry_ref[e], 0.0)
        planes.append(total)
    tab_ref[...] = jnp.concatenate(planes + [jnp.zeros((32, 101), F32)], axis=1).astype(BF16)
    hots[me] = hot_ref[...]
    tabs[my_slab] = tab_ref[...]
    loads[0].wait()
    loads[1].wait()
    pair = jnp.concatenate([img_ref[0].astype(BF16), img_ref[1].astype(BF16)], axis=1)
    first = jnp.dot(pair, w1_ref[...], preferred_element_type=F32).astype(BF16)
    hbuf[0:BOX, :] = first[:, :BOX]
    hbuf[BOX:, :] = first[:, BOX:]

    pl.semaphore_wait(barrier, DEVS - 1)

    def hot_copy(slot, d):
        return pltpu.make_async_remote_copy(
            src_ref=hot_ref, dst_ref=hots.at[slot], send_sem=hot_send.at[d], recv_sem=hot_recv.at[slot],
            device_id=where_is(d), device_id_type=MESH)

    def tab_copy(slot):
        return pltpu.make_async_remote_copy(
            src_ref=tab_ref, dst_ref=tabs.at[slot], send_sem=tab_send, recv_sem=tab_recv,
            device_id=where_is(me + 2 - 4 * my_slab), device_id_type=MESH)

    def g_copy(slot, d):
        return pltpu.make_async_remote_copy(
            src_ref=gbuf.at[d], dst_ref=rbuf.at[slot], send_sem=g_send.at[d], recv_sem=g_recv.at[slot],
            device_id=where_is(d), device_id_type=MESH)

    def z_copy(slot, d):
        return pltpu.make_async_remote_copy(
            src_ref=zbuf.at[d], dst_ref=zrecv.at[slot], send_sem=z_send.at[d], recv_sem=z_recv.at[slot],
            device_id=where_is(d), device_id_type=MESH)

    tab_copy(my_slab).start()
    for n in range(1, DEVS):
        hot_copy(me, peer(n)).start()

    loads[2].wait()
    my_quad = me // 4
    my_place = me % 4
    for step in (2, 1, 3, 0):
        quad = (my_quad + step) % 4
        rows = w2_ref[pl.ds(pl.multiple_of(quad * 192, 192), 192), :]
        made = jnp.dot(rows, hbuf[...], preferred_element_type=F32).astype(BF16)
        gbuf[pl.ds(quad * 4, 4)] = made.reshape(4, 2 * ROWS, BOX)
        for n in range(4 if step else 3):
            d = quad * 4 + (n if step else (my_place + 1 + n) % 4)
            g_copy(me, d).start()
    rbuf[me] = gbuf[me]

    loads[3].wait()
    tab_copy(1 - my_slab).wait()
    for n in range(1, DEVS):
        hot_copy(peer(n), peer(n)).wait()
    hot = jnp.concatenate([hots[:, 0, :], hots[:, 1, :]], axis=0)[:, :32].astype(BF16)
    chosen = jnp.concatenate(
        [jnp.dot(hot, tabs[s], preferred_element_type=F32).astype(BF16) for s in range(2)], axis=1)
    mixed = jnp.concatenate(
        [jnp.dot(chosen, place_ref[n], preferred_element_type=F32).astype(BF16) for n in range(FREQS)], axis=0)
    lane = lax.broadcasted_iota(jnp.int32, (32, BOX), 1)
    entry = lax.broadcasted_iota(jnp.int32, (32, BOX), 0)
    tile = lane // 128
    mirror = jnp.where(lane == 0, 0, (BOX - lane) // 128)
    for ch in range(3):
        for v in range(2):
            ky = ky_of(me, ch * 8 + (4 * v if ch == 1 else 1 - v))
            at = ky // 128 * 3 + tile
            mirror_at = 9 + (BOX - ky) % BOX // 128 * 3 + mirror
            select = ((entry == at) | (entry == mirror_at)).astype(F32).astype(BF16)
            coef[ch, v] = jnp.dot(mixed, select, preferred_element_type=F32)

    for n in range(1, DEVS):
        g_copy(peer(n), peer(n)).wait()
    gf[...] = rbuf[...].astype(F32)

    sub = lax.broadcasted_iota(jnp.int32, (8, BOX), 0)

    def per_group(ch, _):
        base = pl.multiple_of(ch * 8, 8)
        row_zero = jnp.where(ch == 1, 7 - sub, sub) < jnp.where(ch == 1, 4, 1)

        def per_pair(p, sums):
            gr = gf[p, pl.ds(base, 8), :]
            gi = gf[p, pl.ds(base + ROWS, 8), :]
            new = []
            for n in range(FREQS):
                one = jnp.where(row_zero, coef[ch, 1, pl.ds(n * 32 + p, 1), :], coef[ch, 0, pl.ds(n * 32 + p, 1), :])
                two = jnp.where(
                    row_zero, coef[ch, 1, pl.ds(n * 32 + 16 + p, 1), :], coef[ch, 0, pl.ds(n * 32 + 16 + p, 1), :])
                new.append(sums[2 * n] + (one * gr + two * gi))
                new.append(sums[2 * n + 1] + (one * gi - two * gr))
            return tuple(new)

        sums = lax.fori_loop(0, DEVS, per_pair, tuple(jnp.zeros((8, BOX), F32) for _ in range(2 * FREQS)))
        scales = [scale_ref[pl.ds(base + ROWS * j, 8), :] for j in range(4)]
        re = [sums[2 * n] * scales[abs(n - 3)] for n in range(FREQS)]
        im = [sums[2 * n + 1] * scales[abs(n - 3)] for n in range(FREQS)]
        even = [(re[3 + j] + re[3 - j], im[3 + j] + im[3 - j]) for j in range(1, 4)]
        odd = [(re[3 + j] - re[3 - j], im[3 + j] - im[3 - j]) for j in range(1, 4)]
        for o in range(8):
            factor = 0.5 / math.sqrt(6.0) / float(weight[o * 48])
            out_re, out_im = re[3] * factor, im[3] * factor
            for j in range(1, 4):
                c = factor * math.cos(2.0 * math.pi * (j * o % 8) / 8)
                s = factor * math.sin(2.0 * math.pi * (j * o % 8) / 8)
                out_re = out_re + (c * even[j - 1][0] - s * odd[j - 1][1])
                out_im = out_im + (c * even[j - 1][1] + s * odd[j - 1][0])
            qf[ch, o, :, 0:BOX] = out_re
            qf[ch, o, :, BOX:] = out_im
        return 0

    lax.fori_loop(0, 3, per_group, 0)

    loads[4].wait()
    wide = lax.broadcasted_iota(jnp.int32, (8, 2 * BOX), 0)
    own = (wide == 0) & (me == 0)
    sums, diffs = [], []
    for s in range(2):
        for o in range(4 * s, 4 * s + 4):
            a, c = qf[0, o], qf[2, o]
            turned = jnp.concatenate([-c[:, BOX:], c[:, :BOX]], axis=1)
            sums.append(jnp.where(own, a, a + c))
            diffs.append(jnp.where(own, turned, a - c))
        for o in (4 * s, 4 * s + 2):
            a, b = qf[1, o], qf[1, o + 1]
            ra, rb = pltpu.roll(a, 4, axis=0), pltpu.roll(b, 4, axis=0)
            sums.append(jnp.where(wide < 4, a + ra, b + rb))
            diffs.append(jnp.where(wide < 4, a - ra, rb - b))
    real = jnp.dot(jnp.concatenate(sums, axis=0).astype(BF16), w3_ref[0], preferred_element_type=F32)
    imag = jnp.dot(jnp.concatenate(diffs, axis=0).astype(BF16), w3_ref[1], preferred_element_type=F32)
    left = lax.broadcasted_iota(jnp.int32, (96, 128), 1) < 64
    for pair_of in range(4):
        r = real[:, pair_of * 128 : (pair_of + 1) * 128]
        i = imag[:, pair_of * 128 : (pair_of + 1) * 128]
        even_line = jnp.where(left, r, pltpu.roll(i, 64, axis=1)).astype(BF16)
        odd_line = jnp.where(left, pltpu.roll(r, 64, axis=1), i).astype(BF16)
        for s in range(2):
            zbuf[pair_of * 4 + s * 2] = even_line[s * 48 : (s + 1) * 48]
            zbuf[pair_of * 4 + s * 2 + 1] = odd_line[s * 48 : (s + 1) * 48]
    for n in (8, 7, 9, 6, 10, 5, 11, 4, 12, 3, 13, 2, 14, 1, 15):
        z_copy(me, peer(n)).start()
    zrecv[me] = zbuf[me]
    loads[5].wait()
    for n in range(1, DEVS):
        z_copy(peer(n), peer(n)).wait()
    got = zrecv[...].astype(F32)
    for o in range(4):
        shared = 32 + o // 2 * 8
        column = jnp.concatenate(
            [got[:, o * 8 : o * 8 + 8, :].reshape(128, 128), got[:, shared : shared + 8, :].reshape(128, 128)],
            axis=0).astype(BF16)
        res = lax.dot_general(column, w4_ref[o % 2], (((0,), (0,)), ((), ())), preferred_element_type=F32)
        out_ref[o] = res[0:XS, :BOX] - res[64 : 64 + XS, BOX:]


def fused(images, poses, plane_index, plane_weight, shell_counts):
    tables, weight = host_tables()
    vmem = pl.BlockSpec(memory_space=pltpu.VMEM)
    scale = pl.pallas_call(
        scale_kernel,
        out_shape=jax.ShapeDtypeStruct((4 * ROWS, BOX), F32),
        in_specs=[vmem],
        out_specs=vmem,
        name="shell_scale",
    )(shell_counts.reshape(1, -1))
    whole = pl.BlockSpec(memory_space=pl.ANY)
    index = plane_index[:, 0].transpose(1, 0, 2)
    entries = plane_weight[:, 0].transpose(1, 0, 2)
    return pl.pallas_call(
        functools.partial(main_kernel, weight),
        out_shape=jax.ShapeDtypeStruct((4, XS, BOX), F32),
        in_specs=[whole, pl.BlockSpec(memory_space=pltpu.SMEM), vmem, vmem, vmem] + [whole] * 5,
        out_specs=vmem,
        scratch_shapes=[
            pltpu.VMEM(images.shape, F32),
            *[pltpu.VMEM(t.shape, BF16) for t in tables],
            pltpu.VMEM((8, 128), F32),
            pltpu.VMEM((32, 128), BF16),
            pltpu.VMEM((DEVS, 8, 128), F32),
            pltpu.VMEM((2, 32, 128), BF16),
            pltpu.VMEM((2 * BOX, BOX), BF16),
            pltpu.VMEM((DEVS, 2 * ROWS, BOX), BF16),
            pltpu.VMEM((DEVS, 2 * ROWS, BOX), BF16),
            pltpu.VMEM((DEVS, 2 * ROWS, BOX), F32),
            pltpu.VMEM((3, 2, FREQS * 32, BOX), F32),
            pltpu.VMEM((3, 8, 8, 2 * BOX), F32),
            pltpu.VMEM((DEVS, 48, 128), BF16),
            pltpu.VMEM((DEVS, 48, 128), BF16),
            pltpu.SemaphoreType.DMA((DEVS,)),
            pltpu.SemaphoreType.DMA((DEVS,)),
            pltpu.SemaphoreType.DMA,
            pltpu.SemaphoreType.DMA,
            pltpu.SemaphoreType.DMA((DEVS,)),
            pltpu.SemaphoreType.DMA((DEVS,)),
            pltpu.SemaphoreType.DMA((DEVS,)),
            pltpu.SemaphoreType.DMA((DEVS,)),
            pltpu.SemaphoreType.DMA((6,)),
        ],
        compiler_params=pltpu.CompilerParams(
            collective_id=0, has_side_effects=True, vmem_limit_bytes=48 * 2**20
        ),
        name="reconstruct",
    )(images, poses, index, entries, scale, *[jnp.asarray(t) for t in tables])


def solution(mesh):
    small = (mesh.shape["particle"], mesh.shape["slab"], mesh.shape["rep"]) == (4, 2, 2)
    in_specs = (
        P(("groups", "particle", "slab", "rep"), None, None),
        P(("groups", "particle", "slab", "rep")),
        P(None, "slab", None, None),
        P(None, "slab", None, None),
        P("groups"),
    )
    out_specs = P(("groups", "slab"), ("particle", "rep"), None)
    return jax.shard_map(fused if small else body, mesh=mesh, in_specs=in_specs, out_specs=out_specs, check_vma=False)
```

```python
import functools
import math

import jax
import jax.numpy as jnp
import ml_dtypes
import numpy as np
from jax import lax
from jax.experimental import pallas as pl
from jax.experimental.pallas import tpu as pltpu
from jax.sharding import PartitionSpec as P

ZS = 3
OZS = 4
TSIDE = 3


def phase_table(freq_list, positions, box_size):
    product = freq_list[:, None] * positions[None, :] % box_size
    return 2.0 * math.pi / box_size * product.astype(jnp.float32)


def centered(indices, box_size):
    return jnp.where(indices < box_size // 2, indices, indices - box_size)


def shell_index(squared):
    estimate = jnp.floor(jnp.sqrt(squared.astype(jnp.float32))).astype(jnp.int32)
    estimate = estimate - (estimate * estimate > squared).astype(jnp.int32)
    estimate = estimate + ((estimate + 1) * (estimate + 1) <= squared).astype(jnp.int32)
    return estimate


def grid_weight(positions, box_size):
    return jnp.sinc(centered(positions, box_size).astype(jnp.float32) / box_size) ** 2


def spectra_of(pictures, cos_table, sin_table):
    box_size = cos_table.shape[0]
    cos_sin = jnp.concatenate([cos_table, sin_table], axis=1)
    table_pair = jnp.stack([cos_sin, jnp.concatenate([-sin_table, cos_table], axis=1)])

    def single(picture):
        section_one = jnp.dot(picture, cos_sin, preferred_element_type=jnp.float32)
        real_part = section_one[:, :box_size].astype(jnp.bfloat16)
        imag_part = (-section_one[:, box_size:]).astype(jnp.bfloat16)
        stacked = jnp.concatenate([real_part, imag_part], axis=0)
        return jnp.einsum(
            "aky,yx->akx", table_pair, stacked, preferred_element_type=jnp.float32
        ).astype(jnp.bfloat16)

    return lax.map(single, pictures)


def insert_images(running, spectra, pose_piece, local_index, local_weight):
    highest = lax.Precision.HIGHEST
    pose_total = local_index.shape[0]
    entry_total = local_index.shape[1]
    tile_total = local_index.shape[2]
    plane_total = running.shape[0]
    box_size = spectra.shape[-1]
    tile_size = box_size // TSIDE
    count = pose_piece.shape[0]
    onehot = (pose_piece[:, None] == jnp.arange(pose_total, dtype=jnp.int32)[None, :]).astype(
        jnp.float32
    )
    chosen_index = jnp.dot(
        onehot,
        local_index.reshape(pose_total, entry_total * tile_total).astype(jnp.float32),
        precision=highest,
    )
    chosen_weight = jnp.dot(
        onehot, local_weight.reshape(pose_total, entry_total * tile_total), precision=highest
    )
    chosen_index = chosen_index.reshape(count, entry_total, tile_total)
    chosen_weight = chosen_weight.reshape(count, entry_total, tile_total)
    planes = jnp.arange(plane_total).astype(jnp.float32)
    matches = (chosen_index[..., None] == planes).astype(jnp.float32)
    per_plane = jnp.sum(matches * chosen_weight[..., None], axis=1)
    mixing = (
        per_plane.transpose(2, 1, 0).reshape(plane_total, TSIDE, TSIDE, count).astype(jnp.bfloat16)
    )
    tiled = spectra.reshape(count, 2, TSIDE, tile_size, TSIDE, tile_size)
    added = jnp.einsum("zabi,icaybx->zcaybx", mixing, tiled, preferred_element_type=jnp.float32)
    return added.reshape(plane_total, 2, box_size, box_size)


def body(images, poses, plane_index, plane_weight, shell_counts):
    highest = lax.Precision.HIGHEST
    box_size = images.shape[-1]
    slab_index = lax.axis_index("slab")
    slab_total = lax.axis_size("slab")
    pencil_index = lax.axis_index(("particle", "rep"))
    positions = jnp.arange(box_size, dtype=jnp.int32)
    angles = phase_table(positions, positions, box_size)
    root_box = math.sqrt(box_size)
    cos_table = (jnp.cos(angles) / root_box).astype(jnp.bfloat16)
    sin_table = (jnp.sin(angles) / root_box).astype(jnp.bfloat16)
    local_index = plane_index[:, 0]
    local_weight = plane_weight[:, 0]
    empty_window = jnp.zeros((ZS, 2, box_size, box_size), jnp.float32)
    partial_value = insert_images(
        empty_window,
        spectra_of(
            lax.all_gather(images.astype(jnp.bfloat16), "slab", axis=0, tiled=True),
            cos_table,
            sin_table,
        ),
        lax.all_gather(poses, "slab", axis=0, tiled=True),
        local_index,
        local_weight,
    )
    summed = lax.psum_scatter(partial_value, ("particle", "rep"), scatter_dimension=2, tiled=True)
    row_total = summed.shape[2]
    window_planes = ZS * slab_total
    depth_freq = slab_index * ZS + jnp.arange(ZS, dtype=jnp.int32) - window_planes // 2
    row_freq = centered(pencil_index * row_total + jnp.arange(row_total, dtype=jnp.int32), box_size)
    column_freq = centered(positions, box_size)
    inverse_root = 1.0 / jnp.sqrt(shell_counts.astype(jnp.float32))
    shell_ids = jnp.arange(inverse_root.shape[0], dtype=jnp.int32)

    def plane_scale(depth_value):
        squared = depth_value * depth_value + row_freq[:, None] ** 2 + column_freq[None, :] ** 2
        member = (shell_index(squared)[:, :, None] == shell_ids[None, None, :]).astype(jnp.float32)
        return jnp.dot(member, inverse_root, precision=highest)

    shell_scale = lax.map(plane_scale, depth_freq)
    normed = summed * shell_scale[:, None]
    cosine = jnp.cos(angles) / root_box
    sine = jnp.sin(angles) / root_box
    inverse_table = jnp.stack([jnp.stack([cosine, sine]), jnp.stack([-sine, cosine])])
    across = jnp.einsum("zcyk,cakx->zaxy", normed, inverse_table, precision=highest)
    pencils = lax.all_to_all(across, ("particle", "rep"), split_axis=2, concat_axis=3, tiled=True)
    pencil_lines = jnp.einsum("zcxk,caky->zaxy", pencils, inverse_table, precision=highest)
    column_total = pencil_lines.shape[2]
    out_planes = OZS * slab_total
    spacing = box_size // out_planes
    own_rows = slab_index * OZS + jnp.arange(OZS, dtype=jnp.int32)
    depth_angle = phase_table(
        depth_freq, jnp.arange(lax.axis_size("slab") * OZS, dtype=jnp.int32) * spacing, box_size
    )
    depth_cos = jnp.cos(depth_angle) / math.sqrt(window_planes)
    depth_sin = jnp.sin(depth_angle) / math.sqrt(window_planes)
    raw = lax.psum_scatter(
        jnp.einsum("zo,zxy->oxy", depth_cos, pencil_lines[:, 0], precision=highest)
        - jnp.einsum("zo,zxy->oxy", depth_sin, pencil_lines[:, 1], precision=highest),
        "slab",
        scatter_dimension=0,
        tiled=True,
    )
    column_pos = pencil_index * column_total + jnp.arange(column_total, dtype=jnp.int32)
    correction = (
        grid_weight(own_rows * spacing, box_size)[:, None, None]
        * grid_weight(column_pos, box_size)[None, :, None]
        * grid_weight(positions, box_size)[None, None, :]
    )
    return raw / correction


BOX = 384
DEVS = 16
ROWS = BOX // DEVS
LINES = 8
XS = BOX // LINES
FREQS = 7
MESH = pl.DeviceIdType.MESH
F32 = jnp.float32
BF16 = jnp.bfloat16


def ky_of(me, row):
    back = row >= 12
    j = row - 4 * (back & (row < 16)) - 16 * (row >= 16)
    slot = me * 12 + j
    ky = slot + ((slot >= 128) & (slot < 132)) - 4 * (slot == 132)
    return ky + back * (BOX - 2 * ky - (BOX // 2) * (slot == 0))


def host_tables():
    k = np.arange(BOX)
    theta = 2.0 * np.pi * ((k[:, None] * k[None, :]) % BOX) / BOX
    cos, sin = np.cos(theta) / math.sqrt(BOX), np.sin(theta) / math.sqrt(BOX)
    q = np.where(k < BOX // 2, k, k - BOX)
    weight = np.sinc(q / BOX) ** 2
    over_x = np.block([[cos, -sin], [sin, cos]])
    both = np.stack([np.concatenate([cos, sin], 1), np.concatenate([-sin, cos], 1)])
    order = ky_of(np.arange(DEVS)[:, None], np.arange(ROWS)[None, :])
    over_y = both[:, order].transpose(1, 0, 2, 3).reshape(2 * BOX, 2 * BOX)
    def lines(table):
        padded = np.zeros((2 * BOX, LINES, 64))
        padded[:, :, :XS] = (table / weight).reshape(2 * BOX, LINES, XS)
        return padded.reshape(2 * BOX, LINES * 64)

    back_x = np.stack([lines(np.concatenate([cos, -sin], 0)), lines(np.concatenate([sin, cos], 0))])
    positive = order[:, :12]
    parts = [cos[positive] / weight, sin[positive] / weight]
    parts[1][0, 0] = -cos[BOX // 2] / weight
    basis = np.concatenate(parts, 2)
    back_y = np.zeros((2, 2, DEVS, 8, 2 * BOX))
    for parity in range(2):
        back_y[parity, 0] = basis[:, :8]
        back_y[parity, 1, :, 4 * parity : 4 * parity + 4] = basis[:, 8:]
    back_y = back_y.reshape(2, 2 * DEVS * 8, 2 * BOX)
    place = np.zeros((FREQS, 64, 32))
    for n in range(FREQS):
        for side, kz in enumerate((n - 3, 3 - n)):
            if kz <= 2:
                slab, plane = divmod(kz + 3, ZS)
                for t in range(9):
                    place[n, slab * 32 + plane * 9 + t, side * 9 + t] = 1.0
    tables = over_x, over_y, back_x, back_y, place
    return [t.astype(np.float32).astype(ml_dtypes.bfloat16) for t in tables], weight


def device_number():
    return lax.axis_index("particle") * 4 + lax.axis_index("slab") * 2 + lax.axis_index("rep")


def shell_scales(counts_ref, out_ref):
    me = device_number()
    row = lax.broadcasted_iota(jnp.int32, (ROWS, 128), 0)
    back = row >= 12
    slot = me * 12 + jnp.where(back, jnp.where(row < 16, row - 4, row - 16), row)
    ky = jnp.where((slot >= 128) & (slot < 132), slot + 1, jnp.where(slot == 132, 128, slot))
    ky = jnp.where(back & (slot == 0), BOX // 2, ky)
    filled = jnp.concatenate([counts_ref[...].reshape(1, -1), jnp.ones((1, BOX - counts_ref.shape[0]), jnp.int32)], axis=1)
    root = lax.rsqrt(filled.astype(F32))
    for tile in range(3):
        kx = lax.broadcasted_iota(jnp.int32, (ROWS, 128), 1) + tile * 128
        kx = jnp.where(kx < BOX // 2, kx, kx - BOX)
        for kz in range(4):
            r2 = ky * ky + kx * kx + kz * kz
            s = jnp.sqrt(r2.astype(F32)).astype(jnp.int32)
            s = s - (s * s > r2).astype(jnp.int32)
            s = s + ((s + 1) * (s + 1) <= r2).astype(jnp.int32)
            low = s % 128
            total = jnp.zeros((ROWS, 128), F32)
            for part in range(3):
                line = jnp.broadcast_to(root[:, part * 128 : (part + 1) * 128], (ROWS, 128))
                got = jnp.take_along_axis(line, low, axis=1, mode="promise_in_bounds")
                total = jnp.where(s // 128 == part, got, total)
            out_ref[kz * ROWS : (kz + 1) * ROWS, tile * 128 : (tile + 1) * 128] = total


def _nt(left, right):
    return lax.dot_general(left, right, (((1,), (1,)), ((), ())), preferred_element_type=F32)


def main_kernel(
    weight,
    img_hbm, poses_ref, index_ref, entry_ref, counts_ref, w1_hbm, w2_hbm, w3_hbm, w4_hbm, place_hbm,
    out_ref,
    img_ref, w1_ref, w2_ref, w3_ref, w4_ref, place_ref, hot_ref, tab_ref, scale_ref, acc,
    hots, tabs, hbuf, gbuf, rbuf, gf, coef, qf, zbuf, zrecv,
    hot_send, hot_recv, tab_send, tab_recv, g_send, g_recv, z_send, z_recv, load_sem,
):
    me = device_number()
    group = lax.axis_index("groups")
    my_slab = lax.axis_index("slab")

    def where_is(d):
        return (group, d // 4, (d // 2) % 2, d % 2)

    def peer(n):
        return (me + n) % DEVS

    barrier = pltpu.get_barrier_semaphore()
    for n in range(1, DEVS):
        pl.semaphore_signal(barrier, inc=1, device_id=where_is(peer(n)), device_id_type=MESH)

    loads = [
        pltpu.make_async_copy(src, dst, load_sem.at[n])
        for n, (src, dst) in enumerate([
            (img_hbm, img_ref), (w1_hbm, w1_ref), (w2_hbm, w2_ref), (place_hbm, place_ref),
            (w3_hbm, w3_ref), (w4_hbm, w4_ref)])
    ]
    for load in loads:
        load.start()

    spot = lax.broadcasted_iota(jnp.int32, (8, 128), 1)
    line = lax.broadcasted_iota(jnp.int32, (8, 128), 0)
    hot_ref[...] = (spot == jnp.where(line == 0, poses_ref[0], poses_ref[1])).astype(F32)
    planes = []
    for z in range(ZS):
        planes.append(jnp.sum(jnp.where(index_ref[...] == z, entry_ref[...], 0.0), axis=1))
    tab_ref[...] = jnp.concatenate(planes + [jnp.zeros((5, 32), F32)], axis=0).astype(BF16)
    hots[me] = hot_ref[...]
    tabs[my_slab] = tab_ref[...]
    loads[0].wait()
    loads[1].wait()
    pair = jnp.concatenate([img_ref[0].astype(BF16), img_ref[1].astype(BF16)], axis=1)
    first = jnp.dot(pair, w1_ref[...], preferred_element_type=F32).astype(BF16)
    hbuf[0:BOX, :] = first[:, :BOX]
    hbuf[BOX:, :] = first[:, BOX:]

    pl.semaphore_wait(barrier, DEVS - 1)

    def hot_copy(slot, d):
        return pltpu.make_async_remote_copy(
            src_ref=hot_ref, dst_ref=hots.at[slot], send_sem=hot_send.at[d], recv_sem=hot_recv.at[slot],
            device_id=where_is(d), device_id_type=MESH)

    def tab_copy(slot):
        return pltpu.make_async_remote_copy(
            src_ref=tab_ref, dst_ref=tabs.at[slot], send_sem=tab_send, recv_sem=tab_recv,
            device_id=where_is(me + 2 - 4 * my_slab), device_id_type=MESH)

    def g_copy(slot, d):
        return pltpu.make_async_remote_copy(
            src_ref=gbuf.at[d], dst_ref=rbuf.at[slot], send_sem=g_send.at[d], recv_sem=g_recv.at[slot],
            device_id=where_is(d), device_id_type=MESH)

    def z_copy(slot, d):
        return pltpu.make_async_remote_copy(
            src_ref=zbuf.at[d], dst_ref=zrecv.at[slot], send_sem=z_send.at[d], recv_sem=z_recv.at[slot],
            device_id=where_is(d), device_id_type=MESH)

    tab_copy(my_slab).start()
    for n in range(1, DEVS):
        hot_copy(me, peer(n)).start()

    loads[2].wait()
    my_quad = me // 4
    my_place = me % 4
    half, side = my_quad // 2, my_quad % 2
    quads = (2 - 2 * half + side, 3 - 2 * half - side, 2 * half + 1 - side, my_quad)
    for quad in quads:
        rows = w2_ref[pl.ds(pl.multiple_of(quad * 192, 192), 192), :]
        made = jnp.dot(rows, hbuf[...], preferred_element_type=F32).astype(BF16)
        gbuf[pl.ds(quad * 4, 4)] = made.reshape(4, 2 * ROWS, BOX)
        for n in range(3 if quad is my_quad else 4):
            d = quad * 4 + ((my_place + 1 + n) % 4 if quad is my_quad else n)
            g_copy(me, d).start()
    rbuf[me] = gbuf[me]

    shell_scales(counts_ref, scale_ref)

    loads[3].wait()
    tab_copy(1 - my_slab).wait()
    for n in range(1, DEVS):
        hot_copy(peer(n), peer(n)).wait()
    hot = jnp.concatenate([hots[:, 0, :], hots[:, 1, :]], axis=0)[:, :32].astype(BF16)
    chosen = jnp.concatenate(
        [_nt(hot, tabs[s]).astype(BF16) for s in range(2)], axis=1)
    mixed = jnp.concatenate(
        [jnp.dot(chosen, place_ref[n], preferred_element_type=F32).astype(BF16) for n in range(FREQS)], axis=0)
    lane = lax.broadcasted_iota(jnp.int32, (32, BOX), 1)
    entry = lax.broadcasted_iota(jnp.int32, (32, BOX), 0)
    tile = lane // 128
    mirror = jnp.where(lane == 0, 0, (BOX - lane) // 128)
    for ch in range(3):
        for v in range(2):
            ky = ky_of(me, ch * 8 + (4 * v if ch == 1 else 1 - v))
            at = ky // 128 * 3 + tile
            mirror_at = 9 + (BOX - ky) % BOX // 128 * 3 + mirror
            select = ((entry == at) | (entry == mirror_at)).astype(F32).astype(BF16)
            coef[ch, v] = jnp.dot(mixed, select, preferred_element_type=F32)

    sub = lax.broadcasted_iota(jnp.int32, (8, BOX), 0)

    acc[...] = jnp.zeros(acc.shape, F32)
    for quad in (quads[3], quads[2], quads[0], quads[1]):
        for n in range(3 if quad is my_quad else 4):
            d = quad * 4 + ((my_place + 1 + n) % 4 if quad is my_quad else n)
            g_copy(d, d).wait()
        gf[...] = rbuf[pl.ds(quad * 4, 4)].astype(F32)

        def add_group(ch, _):
            base = pl.multiple_of(ch * 8, 8)
            row_zero = jnp.where(ch == 1, 7 - sub, sub) < jnp.where(ch == 1, 4, 1)

            def per_pair(i, sums):
                p = quad * 4 + i
                gr = gf[i, pl.ds(base, 8), :]
                gi = gf[i, pl.ds(base + ROWS, 8), :]
                new = []
                for n in range(FREQS):
                    one = jnp.where(
                        row_zero, coef[ch, 1, pl.ds(n * 32 + p, 1), :], coef[ch, 0, pl.ds(n * 32 + p, 1), :])
                    two = jnp.where(
                        row_zero, coef[ch, 1, pl.ds(n * 32 + 16 + p, 1), :],
                        coef[ch, 0, pl.ds(n * 32 + 16 + p, 1), :])
                    new.append(sums[2 * n] + (one * gr + two * gi))
                    new.append(sums[2 * n + 1] + (one * gi - two * gr))
                return tuple(new)

            sums = lax.fori_loop(0, 4, per_pair, tuple(acc[ch, n] for n in range(2 * FREQS)))
            for n in range(2 * FREQS):
                acc[ch, n] = sums[n]
            return 0

        lax.fori_loop(0, 3, add_group, 0)

    def per_group(ch, _):
        base = pl.multiple_of(ch * 8, 8)
        sums = [acc[ch, n] for n in range(2 * FREQS)]
        scales = [scale_ref[pl.ds(base + ROWS * j, 8), :] for j in range(4)]
        re = [sums[2 * n] * scales[abs(n - 3)] for n in range(FREQS)]
        im = [sums[2 * n + 1] * scales[abs(n - 3)] for n in range(FREQS)]
        even = [(re[3 + j] + re[3 - j], im[3 + j] + im[3 - j]) for j in range(1, 4)]
        odd = [(re[3 + j] - re[3 - j], im[3 + j] - im[3 - j]) for j in range(1, 4)]
        for o in range(8):
            factor = 0.5 / math.sqrt(6.0) / float(weight[o * 48])
            out_re, out_im = re[3] * factor, im[3] * factor
            for j in range(1, 4):
                c = factor * math.cos(2.0 * math.pi * (j * o % 8) / 8)
                s = factor * math.sin(2.0 * math.pi * (j * o % 8) / 8)
                out_re = out_re + (c * even[j - 1][0] - s * odd[j - 1][1])
                out_im = out_im + (c * even[j - 1][1] + s * odd[j - 1][0])
            qf[ch, o, :, 0:BOX] = out_re
            qf[ch, o, :, BOX:] = out_im
        return 0

    lax.fori_loop(0, 3, per_group, 0)

    loads[4].wait()
    wide = lax.broadcasted_iota(jnp.int32, (8, 2 * BOX), 0)
    own = (wide == 0) & (me == 0)
    sums, diffs = [], []
    for s in range(2):
        for o in range(4 * s, 4 * s + 4):
            a, c = qf[0, o], qf[2, o]
            turned = jnp.concatenate([-c[:, BOX:], c[:, :BOX]], axis=1)
            sums.append(jnp.where(own, a, a + c))
            diffs.append(jnp.where(own, turned, a - c))
        for o in (4 * s, 4 * s + 2):
            a, b = qf[1, o], qf[1, o + 1]
            ra, rb = pltpu.roll(a, 4, axis=0), pltpu.roll(b, 4, axis=0)
            sums.append(jnp.where(wide < 4, a + ra, b + rb))
            diffs.append(jnp.where(wide < 4, a - ra, rb - b))
    real = jnp.dot(jnp.concatenate(sums, axis=0).astype(BF16), w3_ref[0], preferred_element_type=F32)
    imag = jnp.dot(jnp.concatenate(diffs, axis=0).astype(BF16), w3_ref[1], preferred_element_type=F32)
    left = lax.broadcasted_iota(jnp.int32, (96, 128), 1) < 64
    for pair_of in range(4):
        r = real[:, pair_of * 128 : (pair_of + 1) * 128]
        i = imag[:, pair_of * 128 : (pair_of + 1) * 128]
        even_line = jnp.where(left, r, pltpu.roll(i, 64, axis=1)).astype(BF16)
        odd_line = jnp.where(left, pltpu.roll(r, 64, axis=1), i).astype(BF16)
        for s in range(2):
            zbuf[pair_of * 4 + s * 2] = even_line[s * 48 : (s + 1) * 48]
            zbuf[pair_of * 4 + s * 2 + 1] = odd_line[s * 48 : (s + 1) * 48]
    for n in (8, 7, 9, 6, 10, 5, 11, 4, 12, 3, 13, 2, 14, 1, 15):
        z_copy(me, peer(n)).start()
    zrecv[me] = zbuf[me]
    loads[5].wait()
    for n in range(1, DEVS):
        z_copy(peer(n), peer(n)).wait()
    got = zrecv[...].astype(F32)
    for o in range(4):
        shared = 32 + o // 2 * 8
        column = jnp.concatenate(
            [got[:, o * 8 : o * 8 + 8, :].reshape(128, 128), got[:, shared : shared + 8, :].reshape(128, 128)],
            axis=0).astype(BF16)
        res = lax.dot_general(column, w4_ref[o % 2], (((0,), (0,)), ((), ())), preferred_element_type=F32)
        out_ref[o] = res[0:XS, :BOX] - res[64 : 64 + XS, BOX:]


def fused(images, poses, plane_index, plane_weight, shell_counts):
    tables, weight = host_tables()
    vmem = pl.BlockSpec(memory_space=pltpu.VMEM)
    whole = pl.BlockSpec(memory_space=pltpu.HBM)
    index = plane_index[:, 0].transpose(2, 1, 0)
    entries = plane_weight[:, 0].transpose(2, 1, 0)
    return pl.pallas_call(
        functools.partial(main_kernel, weight),
        out_shape=jax.ShapeDtypeStruct((4, XS, BOX), F32),
        in_specs=[whole, pl.BlockSpec(memory_space=pltpu.SMEM), vmem, vmem, vmem] + [whole] * 5,
        out_specs=vmem,
        scratch_shapes=[
            pltpu.VMEM(images.shape, F32),
            *[pltpu.VMEM(t.shape, BF16) for t in tables],
            pltpu.VMEM((8, 128), F32),
            pltpu.VMEM((32, 32), BF16),
            pltpu.VMEM((4 * ROWS, BOX), F32),
            pltpu.VMEM((3, 2 * FREQS, 8, BOX), F32),
            pltpu.VMEM((DEVS, 8, 128), F32),
            pltpu.VMEM((2, 32, 32), BF16),
            pltpu.VMEM((2 * BOX, BOX), BF16),
            pltpu.VMEM((DEVS, 2 * ROWS, BOX), BF16),
            pltpu.VMEM((DEVS, 2 * ROWS, BOX), BF16),
            pltpu.VMEM((4, 2 * ROWS, BOX), F32),
            pltpu.VMEM((3, 2, FREQS * 32, BOX), F32),
            pltpu.VMEM((3, 8, 8, 2 * BOX), F32),
            pltpu.VMEM((DEVS, 48, 128), BF16),
            pltpu.VMEM((DEVS, 48, 128), BF16),
            pltpu.SemaphoreType.DMA((DEVS,)),
            pltpu.SemaphoreType.DMA((DEVS,)),
            pltpu.SemaphoreType.DMA,
            pltpu.SemaphoreType.DMA,
            pltpu.SemaphoreType.DMA((DEVS,)),
            pltpu.SemaphoreType.DMA((DEVS,)),
            pltpu.SemaphoreType.DMA((DEVS,)),
            pltpu.SemaphoreType.DMA((DEVS,)),
            pltpu.SemaphoreType.DMA((6,)),
        ],
        compiler_params=pltpu.CompilerParams(
            collective_id=0, has_side_effects=True, vmem_limit_bytes=56 * 2**20
        ),
        name="reconstruct",
    )(images, poses, index, entries, shell_counts, *[jnp.asarray(t) for t in tables])


def solution(mesh):
    small = (mesh.shape["particle"], mesh.shape["slab"], mesh.shape["rep"]) == (4, 2, 2)
    in_specs = (
        P(("groups", "particle", "slab", "rep"), None, None),
        P(("groups", "particle", "slab", "rep")),
        P(None, "slab", None, None),
        P(None, "slab", None, None),
        P("groups"),
    )
    out_specs = P(("groups", "slab"), ("particle", "rep"), None)
    return jax.shard_map(fused if small else body, mesh=mesh, in_specs=in_specs, out_specs=out_specs, check_vma=False)
```
